32 devices in a mesh: shot: 16 (over z, y, core), surf: 2 (over x).
Axes of the slice: x: 2, y: 2, z: 4, core: 2. Of those that a mesh axis runs over, the one named last changes fastest.
Arguments:
- down_data: bfloat16 [128, 16, 1024], P('shot', 'surf'), may hold values from -1.5 to 1.5
- up_data: bfloat16 [16, 512, 1024], P('surf', 'shot'), may hold values from -6 to 6
- taper_len: int32 [512], P('surf'), may hold values from 0 to 511
Outputs:
- multiples: bfloat16 [512, 128, 1024], P('surf', 'shot')
The draws below stay inside these ranges and needn't reach their ends.
All inputs are finite; a program needn't handle non-finite values.
Results may differ from the reference program's by a relative error of at most 0.0082.
Values may be sent and summed in bfloat16 or wider, within the bound.
A program may use at most 128 MiB of HBM per device.

```python
import math
import jax
import jax.numpy as jnp
from jax import lax

NT = 1024
NF = 512
RAMP = 64
K_DEV = 8
R = 512
S = 128
K = 16
N_SURF = 2


def place_ends(array, rng, least, top_value):
    dims = array.shape
    spot = [jax.random.randint(jax.random.fold_in(rng, axis), (), 0, dims[axis]) for axis in range(len(dims))]
    array = array.at[tuple(spot)].set(least)
    longest = dims.index(max(dims))
    spot[longest] = (spot[longest] + 1) % dims[longest]
    return array.at[tuple(spot)].set(top_value)


def steps_of(key, extent, shards, low, high):
    gain = 1.0
    for dim, shards_of in shards:
        draws = jax.random.uniform(jax.random.fold_in(jax.random.fold_in(key, 6), dim), (shards_of,), jnp.float32, low / len(shards), high / len(shards))
        gain = gain * jnp.repeat(jnp.exp(draws), extent[dim] // shards_of).reshape((-1,) + (1,) * (len(extent) - 1 - dim))
    return gain


def centred(own_key, shape, width, limit, cuts=(), kind=jnp.bfloat16):
    level = steps_of(own_key, shape, cuts, -0.22, 0.18) if cuts else 1.0
    array = jax.random.normal(own_key, shape, jnp.float32) * width * level
    return jnp.minimum(jnp.maximum(array, -limit), limit).astype(kind)


def setup_inputs(seed: int = 0) -> dict:
    seeds = jax.random.split(jax.random.key(seed), 4)
    return {
        "down_data": centred(seeds[0], (S, K, NT), K ** -0.5, 1.5, ((0, 16), (1, 2))),
        "up_data": centred(seeds[1], (K, R, NT), 1.0, 6.0, ((0, 2), (1, 16))),
        "taper_len": place_ends(jax.random.randint(seeds[2], (R,), 0, NT // 2), jax.random.fold_in(seeds[2], 1), 0, (NT // 2) - 1).astype(jnp.int32),
    }


def make_tables(samples):
    freqs = samples // 2
    times = jnp.arange(samples, dtype=jnp.int32)
    levels = jnp.arange(freqs, dtype=jnp.int32)
    phase = (levels[:, None] * times[None, :] % samples).astype(jnp.float32) * jnp.float32(2.0 * math.pi / samples)
    cosine = jnp.cos(phase)
    sine = jnp.sin(phase)
    norm_factor = jnp.float32(1.0 / math.sqrt(samples))
    forward_table = (jnp.concatenate([cosine.T, -sine.T], axis=1) * norm_factor).astype(jnp.bfloat16)
    weights = jnp.where(levels == 0, jnp.float32(1.0), jnp.float32(2.0))[:, None]
    inverse_table = (jnp.concatenate([weights * cosine, -weights * sine], axis=0) * norm_factor).astype(jnp.bfloat16)
    return (forward_table, inverse_table)

def reference(down_data, up_data, taper_len):
    forward_table, inverse_table = make_tables(NT)
    down_spec = jnp.dot(down_data.reshape(S * K, NT), forward_table, preferred_element_type=jnp.float32)
    down_spec = down_spec.astype(jnp.bfloat16).reshape(S, K, 2 * NF)
    up_spec = jnp.dot(up_data.reshape(K * R, NT), forward_table, preferred_element_type=jnp.float32)
    up_spec = up_spec.astype(jnp.bfloat16).reshape(K, R, 2 * NF)
    down_real = down_spec[:, :, :NF].astype(jnp.float32)
    down_imag = down_spec[:, :, NF:].astype(jnp.float32)
    rows_block = R // N_SURF
    blocks = up_spec.reshape(K, N_SURF, rows_block, 2 * NF).transpose(1, 0, 2, 3)
    lengths = taper_len.reshape(N_SURF, rows_block)
    sample_pos = jnp.arange(NT, dtype=jnp.float32)

    def one_block(items):
        block, block_len = items
        total = jnp.zeros((rows_block, S, 2 * NF), jnp.float32)
        for group in range(N_SURF):
            low = group * K_DEV
            up_real = block[low:low + K_DEV, :, :NF].astype(jnp.float32)
            up_imag = block[low:low + K_DEV, :, NF:].astype(jnp.float32)
            dr = down_real[:, low:low + K_DEV]
            di = down_imag[:, low:low + K_DEV]
            real_part = jnp.einsum('skf,krf->rsf', dr, up_real) - jnp.einsum('skf,krf->rsf', di, up_imag)
            imag_part = jnp.einsum('skf,krf->rsf', dr, up_imag) + jnp.einsum('skf,krf->rsf', di, up_real)
            partial_g = jnp.concatenate([real_part, imag_part], axis=2).astype(jnp.bfloat16)
            total = total + partial_g.astype(jnp.float32)
        total = total.astype(jnp.bfloat16)
        trace = jnp.dot(total.reshape(rows_block * S, 2 * NF), inverse_table, preferred_element_type=jnp.float32)
        trace = trace.reshape(rows_block, S, NT)
        mute = jnp.clip((sample_pos[None, :] - block_len.astype(jnp.float32)[:, None] + RAMP) / RAMP, 0.0, 1.0)
        return (trace * mute[:, None, :]).astype(jnp.bfloat16)
    result = lax.map(one_block, (blocks, lengths))
    return result.reshape(R, S, NT)
```

```python
import functools
import math

import jax
import jax.numpy as jnp
import ml_dtypes
import numpy as np
from jax import lax
from jax.experimental import pallas as pl
from jax.experimental.pallas import tpu as pltpu
from jax.sharding import PartitionSpec as P

MESH = pl.DeviceIdType.MESH
F32 = jnp.float32
BF16 = jnp.bfloat16
LAG = 2
FG = 16


def make_tables(samples):
    freqs = samples // 2
    levels = np.arange(freqs)
    phase = (levels[:, None] * np.arange(samples)[None, :] % samples) * (2.0 * math.pi / samples)
    cosine, sine = np.cos(phase), np.sin(phase)
    norm = 1.0 / math.sqrt(samples)
    weights = np.where(levels == 0, 1.0, 2.0)[:, None]
    forward_t = np.concatenate([cosine, -sine], axis=0) * norm
    inverse = np.concatenate([weights * cosine, -weights * sine], axis=0) * norm
    return [v.astype(np.float32).astype(ml_dtypes.bfloat16) for v in (forward_t, inverse)]


def spread_matrix(shots, points):
    half = points // 2
    lane = np.arange(shots * points * FG)
    s, kk = lane // (points * FG), (lane // FG) % points
    row = (kk // half) * (shots * half) + s * half + kk % half
    return (np.arange(shots * points)[:, None] == row[None, :]).astype(ml_dtypes.bfloat16)


def line_targets(pos, j):
    out = []
    if pos >= j and pos < 3:
        out.append(pos + 1)
    if pos <= j and pos > 0:
        out.append(pos - 1)
    return out


def sends_of(w):
    v = 3 - w
    out = []
    for j in (1, 0):
        src = "own" if j == w else "big"
        for t in line_targets(w, j):
            out.append((("A", j, 0), abs(w - j), src, "z", t))
        out.append((("A", j, 0), abs(w - j), src, "y", None))
        out.append((("A", j, 0), abs(w - j), src, "c", None))
    for j in (1, 0):
        src = "own" if j == v else "transit"
        out.append((("X", j, 0), abs(v - j), src, "x", None))
        for t in line_targets(v, j):
            out.append((("T", j, 0), abs(v - j), src, "z", 3 - t))
    for j in (1, 0):
        out.append((("B", j, 0), abs(w - j) + 1, "big", "y", None))
        out.append((("B", j, 0), abs(w - j) + 1, "big", "c", None))
    for j in (1, 0):
        out.append((("A", j, 1), abs(w - j) + 1, "big", "c", None))
        out.append((("B", j, 1), abs(w - j) + 2, "big", "c", None))
    return out


def recv_slot(kind, j, yo, sib):
    return {"A": 0, "B": 1}[kind] * 8 + j * 4 + yo * 2 + sib if kind != "T" else 16 + j


def comm_kernel(up_ref, down_ref, ft_ref, spread_ref, t_ref, big, transit, down_all, e_buf, b_buf, u_buf,
                recv, send, down_recv, down_send):
    pieces = up_ref.shape[0]
    x = lax.axis_index("surf")
    b = lax.axis_index("shot")
    z, y, c = b // 4, (b // 2) % 2, b % 2
    w = jnp.where(x == 0, z, 3 - z)

    def dev(xx, ww, yy, cc):
        zz = jnp.where(xx == 0, ww, 3 - ww)
        return (zz * 4 + yy * 2 + cc, xx)

    def target(role, kind, t):
        if kind == "z":
            return dev(x, t, y, c)
        if kind == "y":
            return dev(x, role, 1 - y, c)
        if kind == "c":
            return dev(x, role, y, 1 - c)
        return dev(1 - x, 3 - role, y, c)

    barrier = pltpu.get_barrier_semaphore()
    for role in range(4):
        @pl.when(w == role)
        def _():
            peers = [("y", None), ("c", None), ("x", None)]
            peers += [("z", t) for t in (role - 1, role + 1) if 0 <= t <= 3]
            for kind, t in peers:
                pl.semaphore_signal(barrier, inc=1, device_id=target(role, kind, t), device_id_type=MESH)
            pl.semaphore_wait(barrier, len(peers))

    def slab(kind, j, yo, sib, p):
        if kind == "T":
            return transit.at[j, p]
        ab = 0 if kind == "A" else 1
        yy = y if yo == 0 else 1 - y
        cc = c if sib == 0 else 1 - c
        return big.at[ab, j, p, yy, cc]

    def copy(role, idx, p):
        (kind, j, yo), _, src, how, t = sends_of(role)[idx]
        if src == "own":
            s_ref = up_ref.at[p]
        elif src == "transit":
            s_ref = transit.at[j, p]
        else:
            s_ref = slab(kind, j, yo, 0, p)
        if kind == "T":
            d_ref, slot = transit.at[j, p], 16 + j
        elif kind == "X":
            d_ref, slot = big.at[1, j, p, y, c], recv_slot("B", j, 0, 0)
        elif how == "y":
            d_ref, slot = s_dst(kind, j, p, y, c), recv_slot(kind, j, 1, 0)
        elif how == "c":
            yy = y if yo == 0 else 1 - y
            d_ref, slot = s_dst(kind, j, p, yy, c), recv_slot(kind, j, yo, 1)
        else:
            d_ref, slot = s_dst(kind, j, p, y, c), recv_slot(kind, j, 0, 0)
        return pltpu.make_async_remote_copy(
            src_ref=s_ref, dst_ref=d_ref, send_sem=send.at[idx, p], recv_sem=recv.at[slot, p],
            device_id=target(role, how, t), device_id_type=MESH)

    def s_dst(kind, j, p, yy, cc):
        return big.at[0 if kind == "A" else 1, j, p, yy, cc]

    def arrived(kind, j, yo, sib, p):
        ref = slab(kind, j, yo, sib, p)
        pltpu.make_async_copy(ref, ref, recv.at[recv_slot(kind, j, yo, sib), p]).wait()

    down_copy = pltpu.make_async_remote_copy(
        src_ref=down_ref, dst_ref=down_all.at[1], send_sem=down_send.at[0], recv_sem=down_recv.at[0],
        device_id=(b, 1 - x), device_id_type=MESH)
    down_copy.start()

    for role in range(4):
        @pl.when(w == role)
        def _(role=role):
            sends = sends_of(role)
            streams = []
            for i, (stream, depth, src, how, t) in enumerate(sends):
                key = ("T", stream[1], 0) if stream[0] == "X" else stream
                if not streams or streams[-1][0] != key:
                    streams.append((key, depth, src, []))
                streams[-1][3].append(i)
            deepest = max(s[1] for s in streams)

            def round_(q, _):
                for key, depth, src, idxs in streams:
                    p = q - LAG * depth

                    @pl.when((p >= 0) & (p < pieces))
                    def _():
                        if src != "own":
                            arrived(*key, 0, p)
                        for i in idxs:
                            copy(role, i, p).start()
                return 0

            lax.fori_loop(0, pieces + LAG * deepest, round_, 0)
            if role <= 1:
                def keep(p, _):
                    big[0, role, p, pl.ds(y, 1), pl.ds(c, 1)] = up_ref[p][None, None]
                    return 0
                lax.fori_loop(0, pieces, keep, 0)

            def drain(p, _):
                for ab in ("A", "B"):
                    for j in (0, 1):
                        for yo in (0, 1):
                            arrived(ab, j, yo, 1, p)
                for i in range(len(sends)):
                    copy(role, i, p).wait_send()
                return 0
            lax.fori_loop(0, pieces, drain, 0)

    down_all[0] = down_ref[...]
    down_copy.wait()

    samples = ft_ref.shape[0]
    shots, half = down_ref.shape[0], down_ref.shape[1]
    groups = samples // 2 // FG
    points = 2 * half
    nt = (((1,), (1,)), ((), ()))
    flat = down_all[...].reshape(points * shots, samples)
    e_buf[...] = lax.dot_general(ft_ref[...], flat, nt, preferred_element_type=F32).astype(BF16)
    wide = points * FG
    mask = (lax.broadcasted_iota(jnp.int32, (256, shots * wide), 0) % FG
            == lax.broadcasted_iota(jnp.int32, (256, shots * wide), 1) % FG)

    def spread(i, _):
        rows = pl.ds(pl.multiple_of(i * 256, 256), 256)
        val = jnp.dot(e_buf[rows, :], spread_ref[...], preferred_element_type=F32)
        b_buf[rows, :] = jnp.where(mask, val, 0.0).astype(BF16)
        return 0
    lax.fori_loop(0, samples // 256, spread, 0)

    def forward(i, _):
        ab, kp = i // (half // 2), i % (half // 2)
        for j in (0, 1):
            rows = big[ab, j, pl.ds(2 * kp, 2)].reshape(256, samples)
            for m in range(2):
                res = lax.dot_general(ft_ref[pl.ds(512 * m, 512), :], rows, nt, preferred_element_type=F32)
                res = res.astype(BF16).reshape(groups, FG, 256)
                for n in range(2):
                    u_buf[:, m, ab * half + 2 * kp + n, :, 128 * j:128 * (j + 1)] = res[:, :, 128 * n:128 * (n + 1)]
        return 0
    lax.fori_loop(0, half, forward, 0)

    first = jnp.where(x == 0, 0, 1)

    def contract(g, _):
        re = b_buf[pl.ds(pl.multiple_of(g * FG, FG), FG), :]
        im = b_buf[pl.ds(pl.multiple_of(samples // 2 + g * FG, FG), FG), :]
        blocks = []
        for s in range(shots):
            r_s, i_s = re[:, wide * s:wide * (s + 1)], im[:, wide * s:wide * (s + 1)]
            blocks.append(jnp.concatenate([r_s, -i_s], axis=1))
            blocks.append(jnp.concatenate([i_s, r_s], axis=1))
        weights = jnp.concatenate(blocks, axis=0)
        u_g = u_buf[g].reshape(2 * wide, 256)
        res = jnp.dot(weights, u_g, preferred_element_type=F32).astype(BF16).reshape(shots, 2, FG, 256)
        t_ref[first, :, :, g] = res[..., :128]
        t_ref[1 - first, :, :, g] = res[..., 128:]
        return 0
    lax.fori_loop(0, groups, contract, 0)


def inverse_kernel(t_ref, inv_ref, len_ref, out_ref, xt):
    step = pl.program_id(1)
    shots = t_ref.shape[1]
    samples = inv_ref.shape[0]
    cols = inv_ref.shape[1]
    ramp = samples // 16

    @pl.when(step == 0)
    def _():
        parts = [t_ref[0, s].astype(F32).T for s in range(shots)]
        xt[...] = jnp.swapaxes(jnp.stack(parts, axis=0), 0, 1).astype(BF16)

    res = jnp.dot(xt[...].reshape(128 * shots, samples), inv_ref[...], preferred_element_type=F32)
    pos = (lax.broadcasted_iota(jnp.int32, (128, cols), 1) + step * cols).astype(F32)
    mute = jnp.clip((pos - len_ref[...].astype(F32) + ramp) / ramp, 0.0, 1.0)
    out_ref[...] = (res.reshape(128, shots, cols) * mute[:, None, :]).astype(BF16)


def fused_body(down_data, up_data, taper_len):
    points_half, rows, samples = up_data.shape
    shots = down_data.shape[0]
    points = 2 * points_half
    ft, inv = make_tables(samples)
    groups = samples // 2 // FG
    vmem = pl.BlockSpec(memory_space=pltpu.VMEM)
    n_send = max(len(sends_of(w)) for w in range(4))
    total = pl.pallas_call(
        comm_kernel,
        out_shape=jax.ShapeDtypeStruct((2, shots, 2, groups, FG, 128), BF16),
        in_specs=[vmem] * 4,
        out_specs=vmem,
        scratch_shapes=[
            pltpu.VMEM((2, 2, points_half, 2, 2, rows, samples), BF16),
            pltpu.VMEM((2, points_half, rows, samples), BF16),
            pltpu.VMEM((2, shots, points_half, samples), BF16),
            pltpu.VMEM((samples, shots * points), BF16),
            pltpu.VMEM((samples, shots * points * FG), BF16),
            pltpu.VMEM((groups, 2, points, FG, 256), BF16),
            pltpu.SemaphoreType.DMA((18, points_half)),
            pltpu.SemaphoreType.DMA((n_send, points_half)),
            pltpu.SemaphoreType.DMA((1,)),
            pltpu.SemaphoreType.DMA((1,)),
        ],
        compiler_params=pltpu.CompilerParams(
            collective_id=0, has_side_effects=True, vmem_limit_bytes=56 * 2**20),
        cost_estimate=pl.CostEstimate(flops=12 * 10**9, bytes_accessed=2**24, transcendentals=0),
    )(up_data, down_data, jnp.asarray(ft), jnp.asarray(spread_matrix(shots, points)))
    total = total.reshape(2, shots, samples, 128)
    cols = 256
    return pl.pallas_call(
        inverse_kernel,
        out_shape=jax.ShapeDtypeStruct((256, shots, samples), BF16),
        grid=(2, samples // cols),
        in_specs=[
            pl.BlockSpec((1, shots, samples, 128), lambda i, t: (i, 0, 0, 0)),
            pl.BlockSpec((samples, cols), lambda i, t: (0, t)),
            pl.BlockSpec((128, 1), lambda i, t: (i, 0)),
        ],
        out_specs=pl.BlockSpec((128, shots, cols), lambda i, t: (i, 0, t)),
        scratch_shapes=[pltpu.VMEM((128, shots, samples), BF16)],
        compiler_params=pltpu.CompilerParams(vmem_limit_bytes=48 * 2**20),
        cost_estimate=pl.CostEstimate(flops=43 * 10**8, bytes_accessed=2**23, transcendentals=0),
    )(total, jnp.asarray(inv), taper_len[:, None])


def plain_body(down_data, up_data, taper_len):
    shots, points, samples = down_data.shape
    freqs = samples // 2
    ft, inv = make_tables(samples)
    forward_table, inverse_table = jnp.asarray(ft).T, jnp.asarray(inv)

    def spectra(data):
        flat = jnp.dot(data.reshape(-1, samples), forward_table, preferred_element_type=F32)
        flat = flat.astype(BF16).reshape(data.shape)
        return flat[:, :, :freqs], flat[:, :, freqs:]

    mul = functools.partial(jnp.einsum, "skf,krf->rsf", preferred_element_type=F32)
    dr, di = spectra(down_data)
    ur, ui = (lax.all_gather(u, "shot", axis=1, tiled=True) for u in spectra(up_data))
    partial = jnp.concatenate([mul(dr, ur) - mul(di, ui), mul(dr, ui) + mul(di, ur)], axis=2)
    total = lax.psum_scatter(partial.astype(BF16), "surf", scatter_dimension=0, tiled=True)
    trace = jnp.einsum("rsf,ft->rst", total, inverse_table, preferred_element_type=F32)
    ramp = samples // 16
    pos = jnp.arange(samples, dtype=F32)
    mute = jnp.clip((pos[None, :] - taper_len.astype(F32)[:, None] + ramp) / ramp, 0.0, 1.0)
    return (trace * mute[:, None, :]).astype(BF16)


def solution(mesh):
    placed = (P("shot", "surf", None), P("surf", "shot", None), P("surf"))
    fits = mesh.shape["shot"] == 16 and mesh.shape["surf"] == 2
    return jax.shard_map(
        fused_body if fits else plain_body,
        mesh=mesh, in_specs=placed, out_specs=P("surf", "shot", None), check_vma=False)
```

```python
import functools
import math

import jax
import jax.numpy as jnp
import ml_dtypes
import numpy as np
from jax import lax
from jax.experimental import pallas as pl
from jax.experimental.pallas import tpu as pltpu
from jax.sharding import PartitionSpec as P

MESH = pl.DeviceIdType.MESH
F32 = jnp.float32
BF16 = jnp.bfloat16
LAG = 1
SPREAD_AT = 3
ROWS = 64
FG = 16


def make_tables(samples):
    freqs = samples // 2
    levels = np.arange(freqs)
    phase = (levels[:, None] * np.arange(samples)[None, :] % samples) * (2.0 * math.pi / samples)
    cosine, sine = np.cos(phase), np.sin(phase)
    norm = 1.0 / math.sqrt(samples)
    weights = np.where(levels == 0, 1.0, 2.0)[:, None]
    forward_t = np.concatenate([cosine, -sine], axis=0) * norm
    inverse = np.concatenate([weights * cosine, -weights * sine], axis=0) * norm
    return [v.astype(np.float32).astype(ml_dtypes.bfloat16) for v in (forward_t, inverse)]


def spread_matrix(shots, points):
    half = points // 2
    lane = np.arange(shots * points * FG)
    s, kk = lane // (points * FG), (lane // FG) % points
    row = (kk // half) * (shots * half) + s * half + kk % half
    return (np.arange(shots * points)[:, None] == row[None, :]).astype(ml_dtypes.bfloat16)


def line_targets(pos, j):
    out = []
    if pos >= j and pos < 3:
        out.append(pos + 1)
    if pos <= j and pos > 0:
        out.append(pos - 1)
    return out


def sends_of(w):
    v = 3 - w
    out = []
    for j in (1, 0):
        src = "own" if j == w else "big"
        for t in line_targets(w, j):
            out.append((("A", j, 0), abs(w - j), src, "z", t))
        out.append((("A", j, 0), abs(w - j), src, "y", None))
        out.append((("A", j, 0), abs(w - j), src, "c", None))
    for j in (1, 0):
        src = "own" if j == v else "transit"
        out.append((("X", j, 0), abs(v - j), src, "x", None))
        for t in line_targets(v, j):
            out.append((("T", j, 0), abs(v - j), src, "z", 3 - t))
    for j in (1, 0):
        out.append((("B", j, 0), abs(w - j) + 1, "big", "y", None))
        out.append((("B", j, 0), abs(w - j) + 1, "big", "c", None))
    for j in (1, 0):
        out.append((("A", j, 1), abs(w - j) + 1, "big", "c", None))
        out.append((("B", j, 1), abs(w - j) + 2, "big", "c", None))
    return out


def recv_slot(kind, j, yo, sib):
    return {"A": 0, "B": 1}[kind] * 8 + j * 4 + yo * 2 + sib if kind != "T" else 16 + j


def comm_kernel(up_ref, down_ref, ft_ref, spread_ref, t_ref, big, transit, down_all, e_buf, b_buf, u_buf, xf,
                recv, send, down_recv, down_send):
    pieces = up_ref.shape[0]
    x = lax.axis_index("surf")
    b = lax.axis_index("shot")
    z, y, c = b // 4, (b // 2) % 2, b % 2
    w = jnp.where(x == 0, z, 3 - z)

    def dev(xx, ww, yy, cc):
        zz = jnp.where(xx == 0, ww, 3 - ww)
        return (zz * 4 + yy * 2 + cc, xx)

    def target(role, kind, t):
        if kind == "z":
            return dev(x, t, y, c)
        if kind == "y":
            return dev(x, role, 1 - y, c)
        if kind == "c":
            return dev(x, role, y, 1 - c)
        return dev(1 - x, 3 - role, y, c)

    barrier = pltpu.get_barrier_semaphore()
    for role in range(4):
        @pl.when(w == role)
        def _():
            peers = [("y", None), ("c", None), ("x", None)]
            peers += [("z", t) for t in (role - 1, role + 1) if 0 <= t <= 3]
            for kind, t in peers:
                pl.semaphore_signal(barrier, inc=1, device_id=target(role, kind, t), device_id_type=MESH)
            pl.semaphore_wait(barrier, len(peers))

    def slab(kind, j, yo, sib, p):
        if kind == "T":
            return transit.at[j, p]
        ab = 0 if kind == "A" else 1
        yy = y if yo == 0 else 1 - y
        cc = c if sib == 0 else 1 - c
        return big.at[ab, j, p, yy, cc]

    def copy(role, idx, p):
        (kind, j, yo), _, src, how, t = sends_of(role)[idx]
        if src == "own":
            s_ref = up_ref.at[p]
        elif src == "transit":
            s_ref = transit.at[j, p]
        else:
            s_ref = slab(kind, j, yo, 0, p)
        if kind == "T":
            d_ref, slot = transit.at[j, p], 16 + j
        elif kind == "X":
            d_ref, slot = big.at[1, j, p, y, c], recv_slot("B", j, 0, 0)
        elif how == "y":
            d_ref, slot = s_dst(kind, j, p, y, c), recv_slot(kind, j, 1, 0)
        elif how == "c":
            yy = y if yo == 0 else 1 - y
            d_ref, slot = s_dst(kind, j, p, yy, c), recv_slot(kind, j, yo, 1)
        else:
            d_ref, slot = s_dst(kind, j, p, y, c), recv_slot(kind, j, 0, 0)
        return pltpu.make_async_remote_copy(
            src_ref=s_ref, dst_ref=d_ref, send_sem=send.at[idx, p], recv_sem=recv.at[slot, p],
            device_id=target(role, how, t), device_id_type=MESH)

    def s_dst(kind, j, p, yy, cc):
        return big.at[0 if kind == "A" else 1, j, p, yy, cc]

    def arrived(kind, j, yo, sib, p):
        ref = slab(kind, j, yo, sib, p)
        pltpu.make_async_copy(ref, ref, recv.at[recv_slot(kind, j, yo, sib), p]).wait()

    down_copy = pltpu.make_async_remote_copy(
        src_ref=down_ref, dst_ref=down_all.at[1], send_sem=down_send.at[0], recv_sem=down_recv.at[0],
        device_id=(b, 1 - x), device_id_type=MESH)
    down_copy.start()

    samples = ft_ref.shape[0]
    shots, half = down_ref.shape[0], down_ref.shape[1]
    groups = samples // 2 // FG
    points = 2 * half
    wide = points * FG
    nt = (((1,), (1,)), ((), ()))

    for role in range(2):
        @pl.when(w == role)
        def _(role=role):
            def keep(p, _):
                big[0, role, p, pl.ds(y, 1), pl.ds(c, 1)] = up_ref[p][None, None]
                return 0
            lax.fori_loop(0, pieces, keep, 0)

    def relay(role, q):
        streams = []
        for i, (stream, depth, src, how, t) in enumerate(sends_of(role)):
            key = ("T", stream[1], 0) if stream[0] == "X" else stream
            if not streams or streams[-1][0] != key:
                streams.append((key, depth, src, []))
            streams[-1][3].append(i)
        for key, depth, src, idxs in streams:
            p = q - LAG * depth

            @pl.when((p >= 0) & (p < pieces))
            def _():
                if src != "own":
                    arrived(*key, 0, p)
                for i in idxs:
                    copy(role, i, p).start()

    def spread():
        down_all[0] = down_ref[...]
        down_copy.wait()
        flat = down_all[...].reshape(points * shots, samples)
        e_buf[...] = lax.dot_general(ft_ref[...], flat, nt, preferred_element_type=F32).astype(BF16)
        mask = (lax.broadcasted_iota(jnp.int32, (256, shots * wide), 0) % FG
                == lax.broadcasted_iota(jnp.int32, (256, shots * wide), 1) % FG)

        def chunk(i, _):
            rows = pl.ds(pl.multiple_of(i * 256, 256), 256)
            val = jnp.dot(e_buf[rows, :], spread_ref[...], preferred_element_type=F32)
            b_buf[rows, :] = jnp.where(mask, val, 0.0).astype(BF16)
            return 0
        lax.fori_loop(0, samples // 256, chunk, 0)

    def forward(p):
        for ab in (0, 1):
            rows = big[ab, :, pl.ds(p, 1)].reshape(256, samples)
            for m in range(2):
                res = lax.dot_general(ft_ref[pl.ds(512 * m, 512), :], rows, nt, preferred_element_type=F32)
                u_buf[:, m, ab * half + p] = res.astype(BF16).reshape(groups, FG, 256)

    late = LAG * 5 + 1

    def round_(q, _):
        for role in range(4):
            @pl.when(w == role)
            def _(role=role):
                relay(role, q)

        @pl.when(q == SPREAD_AT)
        def _():
            spread()

        p = q - late

        @pl.when(p >= 0)
        def _():
            for ab in ("A", "B"):
                for j in (0, 1):
                    for yo in (0, 1):
                        arrived(ab, j, yo, 1, p)
            forward(p)
        return 0

    lax.fori_loop(0, pieces + late, round_, 0)

    first = jnp.where(x == 0, 0, 1)
    per = 128 // FG

    def contract(gb, _):
        res = []
        for gi in range(per):
            g = gb * per + gi
            re = b_buf[pl.ds(pl.multiple_of(g * FG, FG), FG), :]
            im = b_buf[pl.ds(pl.multiple_of(samples // 2 + g * FG, FG), FG), :]
            blocks = []
            for s in range(shots):
                r_s, i_s = re[:, wide * s:wide * (s + 1)], im[:, wide * s:wide * (s + 1)]
                blocks.append(jnp.concatenate([r_s, -i_s], axis=1))
                blocks.append(jnp.concatenate([i_s, r_s], axis=1))
            weights = jnp.concatenate(blocks, axis=0)
            res.append(jnp.dot(weights, u_buf[g].reshape(2 * wide, 256), preferred_element_type=F32))
        for s in range(shots):
            for cc in range(2):
                at = (s * 2 + cc) * FG
                val = jnp.concatenate([r[at:at + FG] for r in res], axis=0)
                xf[cc, pl.ds(s, 256, stride=shots), :] = val.T
        for cc in range(2):
            lanes = pl.ds(pl.multiple_of(cc * (samples // 2) + gb * 128, 128), 128)
            for j in range(2):
                h = first if j == 0 else 1 - first
                t_ref[pl.ds(pl.multiple_of(h * 128 * shots, 128), 128 * shots), lanes] = (
                    xf[cc, pl.ds(128 * shots * j, 128 * shots), :].astype(BF16))
        return 0
    lax.fori_loop(0, groups // per, contract, 0)

    for role in range(4):
        @pl.when(w == role)
        def _(role=role):
            def drain(p, _):
                for i in range(len(sends_of(role))):
                    copy(role, i, p).wait_send()
                return 0
            lax.fori_loop(0, pieces, drain, 0)


def inverse_kernel(t_ref, inv_ref, len_ref, out_ref):
    rows, shots, samples = out_ref.shape
    ramp = samples // 16
    lens = jnp.broadcast_to(len_ref[...].astype(F32), (rows, len_ref.shape[1]))
    own = (lax.broadcasted_iota(jnp.int32, lens.shape, 1)
           == lax.broadcasted_iota(jnp.int32, lens.shape, 0) + pl.program_id(0) * rows)
    column = jnp.sum(jnp.where(own, lens, 0.0), axis=1, keepdims=True)
    res = jnp.dot(t_ref[...], inv_ref[...], preferred_element_type=F32)
    pos = lax.broadcasted_iota(jnp.int32, (rows, samples), 1).astype(F32)
    mute = jnp.clip((pos - column + ramp) / ramp, 0.0, 1.0)
    out_ref[...] = (res.reshape(rows, shots, samples) * mute[:, None, :]).astype(BF16)


def fused_body(down_data, up_data, taper_len):
    points_half, rows, samples = up_data.shape
    shots = down_data.shape[0]
    points = 2 * points_half
    ft, inv = make_tables(samples)
    groups = samples // 2 // FG
    vmem = pl.BlockSpec(memory_space=pltpu.VMEM)
    n_send = max(len(sends_of(w)) for w in range(4))
    total = pl.pallas_call(
        comm_kernel,
        out_shape=jax.ShapeDtypeStruct((256 * shots, samples), BF16),
        in_specs=[vmem] * 4,
        out_specs=vmem,
        scratch_shapes=[
            pltpu.VMEM((2, 2, points_half, 2, 2, rows, samples), BF16),
            pltpu.VMEM((2, points_half, rows, samples), BF16),
            pltpu.VMEM((2, shots, points_half, samples), BF16),
            pltpu.VMEM((samples, shots * points), BF16),
            pltpu.VMEM((samples, shots * points * FG), BF16),
            pltpu.VMEM((groups, 2, points, FG, 256), BF16),
            pltpu.VMEM((2, 256 * shots, 128), F32),
            pltpu.SemaphoreType.DMA((18, points_half)),
            pltpu.SemaphoreType.DMA((n_send, points_half)),
            pltpu.SemaphoreType.DMA((1,)),
            pltpu.SemaphoreType.DMA((1,)),
        ],
        compiler_params=pltpu.CompilerParams(
            collective_id=0, has_side_effects=True, vmem_limit_bytes=56 * 2**20),
        cost_estimate=pl.CostEstimate(flops=12 * 10**9, bytes_accessed=2**24, transcendentals=0),
    )(up_data, down_data, jnp.asarray(ft), jnp.asarray(spread_matrix(shots, points)))
    return pl.pallas_call(
        inverse_kernel,
        out_shape=jax.ShapeDtypeStruct((256, shots, samples), BF16),
        grid=(256 // ROWS,),
        in_specs=[
            pl.BlockSpec((ROWS * shots, samples), lambda i: (i, 0)),
            pl.BlockSpec((samples, samples), lambda i: (0, 0)),
            pl.BlockSpec((1, 256), lambda i: (0, 0)),
        ],
        out_specs=pl.BlockSpec((ROWS, shots, samples), lambda i: (i, 0, 0)),
        compiler_params=pltpu.CompilerParams(vmem_limit_bytes=48 * 2**20),
        cost_estimate=pl.CostEstimate(flops=43 * 10**8, bytes_accessed=2**23, transcendentals=0),
    )(total, jnp.asarray(inv), taper_len[None, :])


def plain_body(down_data, up_data, taper_len):
    shots, points, samples = down_data.shape
    freqs = samples // 2
    ft, inv = make_tables(samples)
    forward_table, inverse_table = jnp.asarray(ft).T, jnp.asarray(inv)

    def spectra(data):
        flat = jnp.dot(data.reshape(-1, samples), forward_table, preferred_element_type=F32)
        flat = flat.astype(BF16).reshape(data.shape)
        return flat[:, :, :freqs], flat[:, :, freqs:]

    mul = functools.partial(jnp.einsum, "skf,krf->rsf", preferred_element_type=F32)
    dr, di = spectra(down_data)
    ur, ui = (lax.all_gather(u, "shot", axis=1, tiled=True) for u in spectra(up_data))
    partial = jnp.concatenate([mul(dr, ur) - mul(di, ui), mul(dr, ui) + mul(di, ur)], axis=2)
    total = lax.psum_scatter(partial.astype(BF16), "surf", scatter_dimension=0, tiled=True)
    trace = jnp.einsum("rsf,ft->rst", total, inverse_table, preferred_element_type=F32)
    ramp = samples // 16
    pos = jnp.arange(samples, dtype=F32)
    mute = jnp.clip((pos[None, :] - taper_len.astype(F32)[:, None] + ramp) / ramp, 0.0, 1.0)
    return (trace * mute[:, None, :]).astype(BF16)


def solution(mesh):
    placed = (P("shot", "surf", None), P("surf", "shot", None), P("surf"))
    fits = mesh.shape["shot"] == 16 and mesh.shape["surf"] == 2
    return jax.shard_map(
        fused_body if fits else plain_body,
        mesh=mesh, in_specs=placed, out_specs=P("surf", "shot", None), check_vma=False)
```

```python
import functools
import math

import jax
import jax.numpy as jnp
import ml_dtypes
import numpy as np
from jax import lax
from jax.experimental import pallas as pl
from jax.experimental.pallas import tpu as pltpu
from jax.sharding import PartitionSpec as P

MESH = pl.DeviceIdType.MESH
F32 = jnp.float32
BF16 = jnp.bfloat16
LAG = 1
SPREAD_AT = 3
ROWS = 64
FG = 16


def make_tables(samples):
    freqs = samples // 2
    levels = np.arange(freqs)
    phase = (levels[:, None] * np.arange(samples)[None, :] % samples) * (2.0 * math.pi / samples)
    cosine, sine = np.cos(phase), np.sin(phase)
    norm = 1.0 / math.sqrt(samples)
    weights = np.where(levels == 0, 1.0, 2.0)[:, None]
    forward_t = np.concatenate([cosine, -sine], axis=0) * norm
    inverse = np.concatenate([weights * cosine, -weights * sine], axis=0) * norm
    return [v.astype(np.float32).astype(ml_dtypes.bfloat16) for v in (forward_t, inverse)]


def spread_matrix(shots, points):
    half = points // 2
    lane = np.arange(shots * points * FG)
    s, kk = lane // (points * FG), (lane // FG) % points
    row = (kk // half) * (shots * half) + s * half + kk % half
    return (np.arange(shots * points)[:, None] == row[None, :]).astype(ml_dtypes.bfloat16)


def line_targets(pos, j):
    out = []
    if pos >= j and pos < 3:
        out.append(pos + 1)
    if pos <= j and pos > 0:
        out.append(pos - 1)
    return out


VIA_Z = ((0, 2), (1, 0), (2, 2), (4, 4))


def along_z(pos, j, p):
    n = VIA_Z[pos][j]
    return (p % n == n - 1) if n else False


def sends_of(w):
    v = 3 - w
    out = []
    for j in (1, 0):
        src = "own" if j == w else "big"
        for t in line_targets(w, j):
            out.append((("A", j, 0), abs(w - j), src, "z", t))
        out.append((("A", j, 0), abs(w - j), src, "y", None))
        out.append((("A", j, 0), abs(w - j), src, "c", None))
    for j in (1, 0):
        src = "own" if j == v else "transit"
        out.append((("X", j, 0), abs(v - j), src, "x", None))
        for t in line_targets(v, j):
            out.append((("T", j, 0), abs(v - j), src, "z", 3 - t))
    for j in (1, 0):
        out.append((("B", j, 0), abs(w - j) + 1, "big", "y", None))
        out.append((("B", j, 0), abs(w - j) + 1, "big", "c", None))
    for j in (1, 0):
        for t in line_targets(w, j):
            if VIA_Z[t][j]:
                out.append((("A", j, 1), abs(w - j) + 1, "big", "z", t))
        out.append((("A", j, 1), abs(w - j) + 1, "big", "c", None))
        out.append((("B", j, 1), abs(w - j) + 2, "big", "c", None))
    return out


def guard(w, send, p):
    (kind, j, yo), _, _, how, t = send
    if kind == "A" and yo == 1 and how == "z":
        return None if VIA_Z[t][j] == 1 else along_z(t, j, p)
    if kind == "A" and yo == 0 and how == "y" and VIA_Z[w][j]:
        return False if VIA_Z[w][j] == 1 else jnp.logical_not(along_z(w, j, p))
    return None


def when(cond, f):
    if cond is None:
        f()
    elif cond is not False:
        pl.when(cond)(f)


def recv_slot(kind, j, yo, sib):
    return {"A": 0, "B": 1}[kind] * 8 + j * 4 + yo * 2 + sib if kind != "T" else 16 + j


def comm_kernel(up_ref, down_ref, ft_ref, spread_ref, t_ref, big, transit, down_all, e_buf, b_buf, u_buf, xf,
                recv, send, down_recv, down_send):
    pieces = up_ref.shape[0]
    x = lax.axis_index("surf")
    b = lax.axis_index("shot")
    z, y, c = b // 4, (b // 2) % 2, b % 2
    w = jnp.where(x == 0, z, 3 - z)

    def dev(xx, ww, yy, cc):
        zz = jnp.where(xx == 0, ww, 3 - ww)
        return (zz * 4 + yy * 2 + cc, xx)

    def target(role, kind, t):
        if kind == "z":
            return dev(x, t, y, c)
        if kind == "y":
            return dev(x, role, 1 - y, c)
        if kind == "c":
            return dev(x, role, y, 1 - c)
        return dev(1 - x, 3 - role, y, c)

    barrier = pltpu.get_barrier_semaphore()
    for role in range(4):
        @pl.when(w == role)
        def _():
            peers = [("y", None), ("c", None), ("x", None)]
            peers += [("z", t) for t in (role - 1, role + 1) if 0 <= t <= 3]
            for kind, t in peers:
                pl.semaphore_signal(barrier, inc=1, device_id=target(role, kind, t), device_id_type=MESH)
            pl.semaphore_wait(barrier, len(peers))

    def slab(kind, j, yo, sib, p):
        if kind == "T":
            return transit.at[j, p]
        ab = 0 if kind == "A" else 1
        yy = y if yo == 0 else 1 - y
        cc = c if sib == 0 else 1 - c
        return big.at[ab, j, p, yy, cc]

    def copy(role, idx, p):
        (kind, j, yo), _, src, how, t = sends_of(role)[idx]
        if src == "own":
            s_ref = up_ref.at[p]
        elif src == "transit":
            s_ref = transit.at[j, p]
        else:
            s_ref = slab(kind, j, yo, 0, p)
        yy = y if yo == 0 else 1 - y
        if kind == "T":
            d_ref, slot = transit.at[j, p], 16 + j
        elif kind == "X":
            d_ref, slot = big.at[1, j, p, y, c], recv_slot("B", j, 0, 0)
        elif how == "y":
            d_ref, slot = s_dst(kind, j, p, y, c), recv_slot(kind, j, 1, 0)
        elif how == "c":
            d_ref, slot = s_dst(kind, j, p, yy, c), recv_slot(kind, j, yo, 1)
        else:
            d_ref, slot = s_dst(kind, j, p, yy, c), recv_slot(kind, j, yo, 0)
        return pltpu.make_async_remote_copy(
            src_ref=s_ref, dst_ref=d_ref, send_sem=send.at[idx, p], recv_sem=recv.at[slot, p],
            device_id=target(role, how, t), device_id_type=MESH)

    def s_dst(kind, j, p, yy, cc):
        return big.at[0 if kind == "A" else 1, j, p, yy, cc]

    def arrived(kind, j, yo, sib, p):
        ref = slab(kind, j, yo, sib, p)
        pltpu.make_async_copy(ref, ref, recv.at[recv_slot(kind, j, yo, sib), p]).wait()

    down_copy = pltpu.make_async_remote_copy(
        src_ref=down_ref, dst_ref=down_all.at[1], send_sem=down_send.at[0], recv_sem=down_recv.at[0],
        device_id=(b, 1 - x), device_id_type=MESH)
    down_copy.start()

    samples = ft_ref.shape[0]
    shots, half = down_ref.shape[0], down_ref.shape[1]
    groups = samples // 2 // FG
    points = 2 * half
    wide = points * FG
    nt = (((1,), (1,)), ((), ()))

    for role in range(2):
        @pl.when(w == role)
        def _(role=role):
            def keep(p, _):
                big[0, role, p, pl.ds(y, 1), pl.ds(c, 1)] = up_ref[p][None, None]
                return 0
            lax.fori_loop(0, pieces, keep, 0)

    def start(role, i, p):
        copy(role, i, p).start()

    def sent(role, i, p):
        copy(role, i, p).wait_send()

    def relay(role, q):
        streams = []
        for i, (stream, depth, src, how, t) in enumerate(sends_of(role)):
            key = ("T", stream[1], 0) if stream[0] == "X" else stream
            if not streams or streams[-1][0] != key:
                streams.append((key, depth, src, []))
            streams[-1][3].append(i)
        for key, depth, src, idxs in streams:
            p = q - LAG * depth

            @pl.when((p >= 0) & (p < pieces))
            def _():
                if src != "own":
                    arrived(*key, 0, p)
                for i in idxs:
                    when(guard(role, sends_of(role)[i], p), functools.partial(start, role, i, p))

    def spread():
        down_all[0] = down_ref[...]
        down_copy.wait()
        flat = down_all[...].reshape(points * shots, samples)
        e_buf[...] = lax.dot_general(ft_ref[...], flat, nt, preferred_element_type=F32).astype(BF16)
        mask = (lax.broadcasted_iota(jnp.int32, (256, shots * wide), 0) % FG
                == lax.broadcasted_iota(jnp.int32, (256, shots * wide), 1) % FG)

        def chunk(i, _):
            rows = pl.ds(pl.multiple_of(i * 256, 256), 256)
            val = jnp.dot(e_buf[rows, :], spread_ref[...], preferred_element_type=F32)
            b_buf[rows, :] = jnp.where(mask, val, 0.0).astype(BF16)
            return 0
        lax.fori_loop(0, samples // 256, chunk, 0)

    def forward(p):
        for ab in (0, 1):
            rows = big[ab, :, pl.ds(p, 1)].reshape(256, samples)
            for m in range(2):
                res = lax.dot_general(ft_ref[pl.ds(512 * m, 512), :], rows, nt, preferred_element_type=F32)
                u_buf[:, m, ab * half + p] = res.astype(BF16).reshape(groups, FG, 256)

    late = LAG * 5 + 1

    def round_(q, _):
        for role in range(4):
            @pl.when(w == role)
            def _(role=role):
                relay(role, q)

        @pl.when(q == SPREAD_AT)
        def _():
            spread()

        p = q - late

        @pl.when(p >= 0)
        def _():
            for ab in ("A", "B"):
                for j in (0, 1):
                    for yo in (0, 1):
                        arrived(ab, j, yo, 1, p)
            forward(p)
        return 0

    lax.fori_loop(0, pieces + late, round_, 0)

    first = jnp.where(x == 0, 0, 1)
    per = 128 // FG

    def contract(gb, _):
        res = []
        for gi in range(per):
            g = gb * per + gi
            re = b_buf[pl.ds(pl.multiple_of(g * FG, FG), FG), :]
            im = b_buf[pl.ds(pl.multiple_of(samples // 2 + g * FG, FG), FG), :]
            blocks = []
            for s in range(shots):
                r_s, i_s = re[:, wide * s:wide * (s + 1)], im[:, wide * s:wide * (s + 1)]
                blocks.append(jnp.concatenate([r_s, -i_s], axis=1))
                blocks.append(jnp.concatenate([i_s, r_s], axis=1))
            weights = jnp.concatenate(blocks, axis=0)
            res.append(jnp.dot(weights, u_buf[g].reshape(2 * wide, 256), preferred_element_type=F32))
        for s in range(shots):
            for cc in range(2):
                at = (s * 2 + cc) * FG
                val = jnp.concatenate([r[at:at + FG] for r in res], axis=0)
                xf[cc, pl.ds(s, 256, stride=shots), :] = val.T
        for cc in range(2):
            lanes = pl.ds(pl.multiple_of(cc * (samples // 2) + gb * 128, 128), 128)
            for j in range(2):
                h = first if j == 0 else 1 - first
                t_ref[pl.ds(pl.multiple_of(h * 128 * shots, 128), 128 * shots), lanes] = (
                    xf[cc, pl.ds(128 * shots * j, 128 * shots), :].astype(BF16))
        return 0
    lax.fori_loop(0, groups // per, contract, 0)

    for role in range(4):
        @pl.when(w == role)
        def _(role=role):
            def drain(p, _):
                for i, one in enumerate(sends_of(role)):
                    when(guard(role, one, p), functools.partial(sent, role, i, p))
                return 0
            lax.fori_loop(0, pieces, drain, 0)


def inverse_kernel(t_ref, inv_ref, len_ref, out_ref):
    rows, shots, samples = out_ref.shape
    ramp = samples // 16
    lens = jnp.broadcast_to(len_ref[...].astype(F32), (rows, len_ref.shape[1]))
    own = (lax.broadcasted_iota(jnp.int32, lens.shape, 1)
           == lax.broadcasted_iota(jnp.int32, lens.shape, 0) + pl.program_id(0) * rows)
    column = jnp.sum(jnp.where(own, lens, 0.0), axis=1, keepdims=True)
    res = jnp.dot(t_ref[...], inv_ref[...], preferred_element_type=F32)
    pos = lax.broadcasted_iota(jnp.int32, (rows, samples), 1).astype(F32)
    mute = jnp.clip((pos - column + ramp) / ramp, 0.0, 1.0)
    out_ref[...] = (res.reshape(rows, shots, samples) * mute[:, None, :]).astype(BF16)


def fused_body(down_data, up_data, taper_len):
    points_half, rows, samples = up_data.shape
    shots = down_data.shape[0]
    points = 2 * points_half
    ft, inv = make_tables(samples)
    groups = samples // 2 // FG
    vmem = pl.BlockSpec(memory_space=pltpu.VMEM)
    n_send = max(len(sends_of(w)) for w in range(4))
    total = pl.pallas_call(
        comm_kernel,
        out_shape=jax.ShapeDtypeStruct((256 * shots, samples), BF16),
        in_specs=[vmem] * 4,
        out_specs=vmem,
        scratch_shapes=[
            pltpu.VMEM((2, 2, points_half, 2, 2, rows, samples), BF16),
            pltpu.VMEM((2, points_half, rows, samples), BF16),
            pltpu.VMEM((2, shots, points_half, samples), BF16),
            pltpu.VMEM((samples, shots * points), BF16),
            pltpu.VMEM((samples, shots * points * FG), BF16),
            pltpu.VMEM((groups, 2, points, FG, 256), BF16),
            pltpu.VMEM((2, 256 * shots, 128), F32),
            pltpu.SemaphoreType.DMA((18, points_half)),
            pltpu.SemaphoreType.DMA((n_send, points_half)),
            pltpu.SemaphoreType.DMA((1,)),
            pltpu.SemaphoreType.DMA((1,)),
        ],
        compiler_params=pltpu.CompilerParams(
            collective_id=0, has_side_effects=True, vmem_limit_bytes=56 * 2**20),
        cost_estimate=pl.CostEstimate(flops=12 * 10**9, bytes_accessed=2**24, transcendentals=0),
    )(up_data, down_data, jnp.asarray(ft), jnp.asarray(spread_matrix(shots, points)))
    return pl.pallas_call(
        inverse_kernel,
        out_shape=jax.ShapeDtypeStruct((256, shots, samples), BF16),
        grid=(256 // ROWS,),
        in_specs=[
            pl.BlockSpec((ROWS * shots, samples), lambda i: (i, 0)),
            pl.BlockSpec((samples, samples), lambda i: (0, 0)),
            pl.BlockSpec((1, 256), lambda i: (0, 0)),
        ],
        out_specs=pl.BlockSpec((ROWS, shots, samples), lambda i: (i, 0, 0)),
        compiler_params=pltpu.CompilerParams(vmem_limit_bytes=48 * 2**20),
        cost_estimate=pl.CostEstimate(flops=43 * 10**8, bytes_accessed=2**23, transcendentals=0),
    )(total, jnp.asarray(inv), taper_len[None, :])


def plain_body(down_data, up_data, taper_len):
    shots, points, samples = down_data.shape
    freqs = samples // 2
    ft, inv = make_tables(samples)
    forward_table, inverse_table = jnp.asarray(ft).T, jnp.asarray(inv)

    def spectra(data):
        flat = jnp.dot(data.reshape(-1, samples), forward_table, preferred_element_type=F32)
        flat = flat.astype(BF16).reshape(data.shape)
        return flat[:, :, :freqs], flat[:, :, freqs:]

    mul = functools.partial(jnp.einsum, "skf,krf->rsf", preferred_element_type=F32)
    dr, di = spectra(down_data)
    ur, ui = (lax.all_gather(u, "shot", axis=1, tiled=True) for u in spectra(up_data))
    partial = jnp.concatenate([mul(dr, ur) - mul(di, ui), mul(dr, ui) + mul(di, ur)], axis=2)
    total = lax.psum_scatter(partial.astype(BF16), "surf", scatter_dimension=0, tiled=True)
    trace = jnp.einsum("rsf,ft->rst", total, inverse_table, preferred_element_type=F32)
    ramp = samples // 16
    pos = jnp.arange(samples, dtype=F32)
    mute = jnp.clip((pos[None, :] - taper_len.astype(F32)[:, None] + ramp) / ramp, 0.0, 1.0)
    return (trace * mute[:, None, :]).astype(BF16)


def solution(mesh):
    placed = (P("shot", "surf", None), P("surf", "shot", None), P("surf"))
    fits = mesh.shape["shot"] == 16 and mesh.shape["surf"] == 2
    return jax.shard_map(
        fused_body if fits else plain_body,
        mesh=mesh, in_specs=placed, out_specs=P("surf", "shot", None), check_vma=False)
```

```python
import functools
import math

import jax
import jax.numpy as jnp
import ml_dtypes
import numpy as np
from jax import lax
from jax.experimental import pallas as pl
from jax.experimental.pallas import tpu as pltpu
from jax.sharding import PartitionSpec as P

MESH = pl.DeviceIdType.MESH
F32 = jnp.float32
BF16 = jnp.bfloat16
LAG = 1
SPREAD_AT = 3
ROWS = 64
FG = 16


def make_tables(samples):
    freqs = samples // 2
    levels = np.arange(freqs)
    phase = (levels[:, None] * np.arange(samples)[None, :] % samples) * (2.0 * math.pi / samples)
    cosine, sine = np.cos(phase), np.sin(phase)
    norm = 1.0 / math.sqrt(samples)
    weights = np.where(levels == 0, 1.0, 2.0)[:, None]
    forward_t = np.concatenate([cosine, -sine], axis=0) * norm
    inverse = np.concatenate([weights * cosine, -weights * sine], axis=0) * norm
    return [v.astype(np.float32).astype(ml_dtypes.bfloat16) for v in (forward_t, inverse)]


def spread_matrix(shots, points):
    half = points // 2
    lane = np.arange(shots * points * FG)
    s, kk = lane // (points * FG), (lane // FG) % points
    row = (kk // half) * (shots * half) + s * half + kk % half
    return (np.arange(shots * points)[:, None] == row[None, :]).astype(ml_dtypes.bfloat16)


def line_targets(pos, j):
    out = []
    if pos >= j and pos < 3:
        out.append(pos + 1)
    if pos <= j and pos > 0:
        out.append(pos - 1)
    return out


VIA_Z = ((0, 2), (1, 0), (2, 2), (4, 4))


def along_z(pos, j, p):
    n = VIA_Z[pos][j]
    return (p % n == n - 1) if n else False


def sends_of(w):
    v = 3 - w
    out = []
    for j in (1, 0):
        src = "own" if j == v else "transit"
        out.append((("X", j, 0), abs(v - j), src, "x", None))
        for t in line_targets(v, j):
            out.append((("T", j, 0), abs(v - j), src, "z", 3 - t))
    for j in (1, 0):
        src = "own" if j == w else "big"
        for t in line_targets(w, j):
            out.append((("A", j, 0), abs(w - j), src, "z", t))
        out.append((("A", j, 0), abs(w - j), src, "y", None))
        out.append((("A", j, 0), abs(w - j), src, "c", None))
    for j in (1, 0):
        out.append((("B", j, 0), abs(w - j) + 1, "big", "y", None))
        out.append((("B", j, 0), abs(w - j) + 1, "big", "c", None))
    for j in (1, 0):
        for t in line_targets(w, j):
            if VIA_Z[t][j]:
                out.append((("A", j, 1), abs(w - j) + 1, "big", "z", t))
        out.append((("A", j, 1), abs(w - j) + 1, "big", "c", None))
        out.append((("B", j, 1), abs(w - j) + 2, "big", "c", None))
    return out


def guard(w, send, p):
    (kind, j, yo), _, _, how, t = send
    if kind == "A" and yo == 1 and how == "z":
        return None if VIA_Z[t][j] == 1 else along_z(t, j, p)
    if kind == "A" and yo == 0 and how == "y" and VIA_Z[w][j]:
        return False if VIA_Z[w][j] == 1 else jnp.logical_not(along_z(w, j, p))
    return None


def when(cond, f):
    if cond is None:
        f()
    elif cond is not False:
        pl.when(cond)(f)


def recv_slot(kind, j, yo, sib):
    return {"A": 0, "B": 1}[kind] * 8 + j * 4 + yo * 2 + sib if kind != "T" else 16 + j


def comm_kernel(up_ref, down_ref, ft_ref, spread_ref, t_ref, big, transit, down_all, e_buf, b_buf, u_buf, xf,
                recv, send, down_recv, down_send):
    pieces = up_ref.shape[0]
    x = lax.axis_index("surf")
    b = lax.axis_index("shot")
    z, y, c = b // 4, (b // 2) % 2, b % 2
    w = jnp.where(x == 0, z, 3 - z)

    def dev(xx, ww, yy, cc):
        zz = jnp.where(xx == 0, ww, 3 - ww)
        return (zz * 4 + yy * 2 + cc, xx)

    def target(role, kind, t):
        if kind == "z":
            return dev(x, t, y, c)
        if kind == "y":
            return dev(x, role, 1 - y, c)
        if kind == "c":
            return dev(x, role, y, 1 - c)
        return dev(1 - x, 3 - role, y, c)

    barrier = pltpu.get_barrier_semaphore()
    for role in range(4):
        @pl.when(w == role)
        def _():
            peers = [("y", None), ("c", None), ("x", None)]
            peers += [("z", t) for t in (role - 1, role + 1) if 0 <= t <= 3]
            for kind, t in peers:
                pl.semaphore_signal(barrier, inc=1, device_id=target(role, kind, t), device_id_type=MESH)
            pl.semaphore_wait(barrier, len(peers))

    def slab(kind, j, yo, sib, p):
        if kind == "T":
            return transit.at[j, p]
        ab = 0 if kind == "A" else 1
        yy = y if yo == 0 else 1 - y
        cc = c if sib == 0 else 1 - c
        return big.at[ab, j, p, yy, cc]

    def copy(role, idx, p):
        (kind, j, yo), _, src, how, t = sends_of(role)[idx]
        if src == "own":
            s_ref = up_ref.at[p]
        elif src == "transit":
            s_ref = transit.at[j, p]
        else:
            s_ref = slab(kind, j, yo, 0, p)
        yy = y if yo == 0 else 1 - y
        if kind == "T":
            d_ref, slot = transit.at[j, p], 16 + j
        elif kind == "X":
            d_ref, slot = big.at[1, j, p, y, c], recv_slot("B", j, 0, 0)
        elif how == "y":
            d_ref, slot = s_dst(kind, j, p, y, c), recv_slot(kind, j, 1, 0)
        elif how == "c":
            d_ref, slot = s_dst(kind, j, p, yy, c), recv_slot(kind, j, yo, 1)
        else:
            d_ref, slot = s_dst(kind, j, p, yy, c), recv_slot(kind, j, yo, 0)
        return pltpu.make_async_remote_copy(
            src_ref=s_ref, dst_ref=d_ref, send_sem=send.at[idx, p], recv_sem=recv.at[slot, p],
            device_id=target(role, how, t), device_id_type=MESH)

    def s_dst(kind, j, p, yy, cc):
        return big.at[0 if kind == "A" else 1, j, p, yy, cc]

    def arrived(kind, j, yo, sib, p):
        ref = slab(kind, j, yo, sib, p)
        pltpu.make_async_copy(ref, ref, recv.at[recv_slot(kind, j, yo, sib), p]).wait()

    down_copy = pltpu.make_async_remote_copy(
        src_ref=down_ref, dst_ref=down_all.at[1], send_sem=down_send.at[0], recv_sem=down_recv.at[0],
        device_id=(b, 1 - x), device_id_type=MESH)
    down_copy.start()

    samples = ft_ref.shape[0]
    shots, half = down_ref.shape[0], down_ref.shape[1]
    groups = samples // 2 // FG
    points = 2 * half
    wide = points * FG
    nt = (((1,), (1,)), ((), ()))

    for role in range(2):
        @pl.when(w == role)
        def _(role=role):
            def keep(p, _):
                big[0, role, p, pl.ds(y, 1), pl.ds(c, 1)] = up_ref[p][None, None]
                return 0
            lax.fori_loop(0, pieces, keep, 0)

    def start(role, i, p):
        copy(role, i, p).start()

    def sent(role, i, p):
        copy(role, i, p).wait_send()

    def relay(role, q):
        streams = []
        for i, (stream, depth, src, how, t) in enumerate(sends_of(role)):
            key = ("T", stream[1], 0) if stream[0] == "X" else stream
            if not streams or streams[-1][0] != key:
                streams.append((key, depth, src, []))
            streams[-1][3].append(i)
        for key, depth, src, idxs in streams:
            p = q - LAG * depth

            @pl.when((p >= 0) & (p < pieces))
            def _():
                if src != "own":
                    arrived(*key, 0, p)
                for i in idxs:
                    when(guard(role, sends_of(role)[i], p), functools.partial(start, role, i, p))

    def spread():
        down_all[0] = down_ref[...]
        down_copy.wait()
        flat = down_all[...].reshape(points * shots, samples)
        e_buf[...] = lax.dot_general(ft_ref[...], flat, nt, preferred_element_type=F32).astype(BF16)
        mask = (lax.broadcasted_iota(jnp.int32, (256, shots * wide), 0) % FG
                == lax.broadcasted_iota(jnp.int32, (256, shots * wide), 1) % FG)

        def chunk(i, _):
            rows = pl.ds(pl.multiple_of(i * 256, 256), 256)
            val = jnp.dot(e_buf[rows, :], spread_ref[...], preferred_element_type=F32)
            b_buf[rows, :] = jnp.where(mask, val, 0.0).astype(BF16)
            return 0
        lax.fori_loop(0, samples // 256, chunk, 0)

    def forward(p):
        for ab in (0, 1):
            rows = big[ab, :, pl.ds(p, 1)].reshape(256, samples)
            for m in range(2):
                res = lax.dot_general(ft_ref[pl.ds(512 * m, 512), :], rows, nt, preferred_element_type=F32)
                u_buf[:, m, ab * half + p] = res.astype(BF16).reshape(groups, FG, 256)

    late = LAG * 5 + 1

    def round_(q, _):
        for role in range(4):
            @pl.when(w == role)
            def _(role=role):
                relay(role, q)

        @pl.when(q == SPREAD_AT)
        def _():
            spread()

        p = q - late

        @pl.when(p >= 0)
        def _():
            for ab in ("A", "B"):
                for j in (0, 1):
                    for yo in (0, 1):
                        arrived(ab, j, yo, 1, p)
            forward(p)
        return 0

    lax.fori_loop(0, pieces + late, round_, 0)

    first = jnp.where(x == 0, 0, 1)
    per = 128 // FG

    def contract(gb, _):
        res = []
        for gi in range(per):
            g = gb * per + gi
            re = b_buf[pl.ds(pl.multiple_of(g * FG, FG), FG), :]
            im = b_buf[pl.ds(pl.multiple_of(samples // 2 + g * FG, FG), FG), :]
            blocks = []
            for s in range(shots):
                r_s, i_s = re[:, wide * s:wide * (s + 1)], im[:, wide * s:wide * (s + 1)]
                blocks.append(jnp.concatenate([r_s, -i_s], axis=1))
                blocks.append(jnp.concatenate([i_s, r_s], axis=1))
            weights = jnp.concatenate(blocks, axis=0)
            res.append(jnp.dot(weights, u_buf[g].reshape(2 * wide, 256), preferred_element_type=F32))
        for s in range(shots):
            for cc in range(2):
                at = (s * 2 + cc) * FG
                val = jnp.concatenate([r[at:at + FG] for r in res], axis=0)
                xf[cc, pl.ds(s, 256, stride=shots), :] = val.T
        for cc in range(2):
            lanes = pl.ds(pl.multiple_of(cc * (samples // 2) + gb * 128, 128), 128)
            for j in range(2):
                h = first if j == 0 else 1 - first
                t_ref[pl.ds(pl.multiple_of(h * 128 * shots, 128), 128 * shots), lanes] = (
                    xf[cc, pl.ds(128 * shots * j, 128 * shots), :].astype(BF16))
        return 0
    lax.fori_loop(0, groups // per, contract, 0)

    for role in range(4):
        @pl.when(w == role)
        def _(role=role):
            def drain(p, _):
                for i, one in enumerate(sends_of(role)):
                    when(guard(role, one, p), functools.partial(sent, role, i, p))
                return 0
            lax.fori_loop(0, pieces, drain, 0)


def inverse_kernel(t_ref, inv_ref, len_ref, out_ref):
    rows, shots, samples = out_ref.shape
    ramp = samples // 16
    lens = jnp.broadcast_to(len_ref[...].astype(F32), (rows, len_ref.shape[1]))
    own = (lax.broadcasted_iota(jnp.int32, lens.shape, 1)
           == lax.broadcasted_iota(jnp.int32, lens.shape, 0) + pl.program_id(0) * rows)
    column = jnp.sum(jnp.where(own, lens, 0.0), axis=1, keepdims=True)
    res = jnp.dot(t_ref[...], inv_ref[...], preferred_element_type=F32)
    pos = lax.broadcasted_iota(jnp.int32, (rows, samples), 1).astype(F32)
    mute = jnp.clip((pos - column + ramp) / ramp, 0.0, 1.0)
    out_ref[...] = (res.reshape(rows, shots, samples) * mute[:, None, :]).astype(BF16)


def fused_body(down_data, up_data, taper_len):
    points_half, rows, samples = up_data.shape
    shots = down_data.shape[0]
    points = 2 * points_half
    ft, inv = make_tables(samples)
    groups = samples // 2 // FG
    vmem = pl.BlockSpec(memory_space=pltpu.VMEM)
    n_send = max(len(sends_of(w)) for w in range(4))
    total = pl.pallas_call(
        comm_kernel,
        out_shape=jax.ShapeDtypeStruct((256 * shots, samples), BF16),
        in_specs=[vmem] * 4,
        out_specs=vmem,
        scratch_shapes=[
            pltpu.VMEM((2, 2, points_half, 2, 2, rows, samples), BF16),
            pltpu.VMEM((2, points_half, rows, samples), BF16),
            pltpu.VMEM((2, shots, points_half, samples), BF16),
            pltpu.VMEM((samples, shots * points), BF16),
            pltpu.VMEM((samples, shots * points * FG), BF16),
            pltpu.VMEM((groups, 2, points, FG, 256), BF16),
            pltpu.VMEM((2, 256 * shots, 128), F32),
            pltpu.SemaphoreType.DMA((18, points_half)),
            pltpu.SemaphoreType.DMA((n_send, points_half)),
            pltpu.SemaphoreType.DMA((1,)),
            pltpu.SemaphoreType.DMA((1,)),
        ],
        compiler_params=pltpu.CompilerParams(
            collective_id=0, has_side_effects=True, vmem_limit_bytes=56 * 2**20),
        cost_estimate=pl.CostEstimate(flops=12 * 10**9, bytes_accessed=2**24, transcendentals=0),
    )(up_data, down_data, jnp.asarray(ft), jnp.asarray(spread_matrix(shots, points)))
    return pl.pallas_call(
        inverse_kernel,
        out_shape=jax.ShapeDtypeStruct((256, shots, samples), BF16),
        grid=(256 // ROWS,),
        in_specs=[
            pl.BlockSpec((ROWS * shots, samples), lambda i: (i, 0)),
            pl.BlockSpec((samples, samples), lambda i: (0, 0)),
            pl.BlockSpec((1, 256), lambda i: (0, 0)),
        ],
        out_specs=pl.BlockSpec((ROWS, shots, samples), lambda i: (i, 0, 0)),
        compiler_params=pltpu.CompilerParams(vmem_limit_bytes=48 * 2**20),
        cost_estimate=pl.CostEstimate(flops=43 * 10**8, bytes_accessed=2**23, transcendentals=0),
    )(total, jnp.asarray(inv), taper_len[None, :])


def plain_body(down_data, up_data, taper_len):
    shots, points, samples = down_data.shape
    freqs = samples // 2
    ft, inv = make_tables(samples)
    forward_table, inverse_table = jnp.asarray(ft).T, jnp.asarray(inv)

    def spectra(data):
        flat = jnp.dot(data.reshape(-1, samples), forward_table, preferred_element_type=F32)
        flat = flat.astype(BF16).reshape(data.shape)
        return flat[:, :, :freqs], flat[:, :, freqs:]

    mul = functools.partial(jnp.einsum, "skf,krf->rsf", preferred_element_type=F32)
    dr, di = spectra(down_data)
    ur, ui = (lax.all_gather(u, "shot", axis=1, tiled=True) for u in spectra(up_data))
    partial = jnp.concatenate([mul(dr, ur) - mul(di, ui), mul(dr, ui) + mul(di, ur)], axis=2)
    total = lax.psum_scatter(partial.astype(BF16), "surf", scatter_dimension=0, tiled=True)
    trace = jnp.einsum("rsf,ft->rst", total, inverse_table, preferred_element_type=F32)
    ramp = samples // 16
    pos = jnp.arange(samples, dtype=F32)
    mute = jnp.clip((pos[None, :] - taper_len.astype(F32)[:, None] + ramp) / ramp, 0.0, 1.0)
    return (trace * mute[:, None, :]).astype(BF16)


def solution(mesh):
    placed = (P("shot", "surf", None), P("surf", "shot", None), P("surf"))
    fits = mesh.shape["shot"] == 16 and mesh.shape["surf"] == 2
    return jax.shard_map(
        fused_body if fits else plain_body,
        mesh=mesh, in_specs=placed, out_specs=P("surf", "shot", None), check_vma=False)
```
